32 devices in a mesh: dp: 4 (over y, x), expert: 8 (over z, core).
Axes of the slice: x: 2, y: 2, z: 4, core: 2. Of those that a mesh axis runs over, the one named last changes fastest.
Arguments:
- tokens: bfloat16 [4096, 4096], P(('dp', 'expert')), may hold values from -6 to 6
- out_grad: bfloat16 [4096, 4096], P(('dp', 'expert')), may hold values from -6 to 6
- expert_ids: int32 [4096, 8], P(('dp', 'expert')), may hold values from 0 to 127, all different within a row; in each aligned block of 128 rows (0 to 127, 128 to 255, ...) at most 9 rows name the same one
- gate_weights: float32 [4096, 8], P(('dp', 'expert')), may hold values from 0.1 to 1
- w_gate: bfloat16 [8, 4096, 1536], P('expert', None, 'dp'), may hold values from -0.09375 to 0.09375
- w_up: bfloat16 [8, 4096, 1536], P('expert', None, 'dp'), may hold values from -0.09375 to 0.09375
- w_down: bfloat16 [8, 1536, 4096], P('expert', 'dp'), may hold values from -0.15625 to 0.15625
Outputs:
- token_grad: bfloat16 [4096, 4096], P(('dp', 'expert'))
- gate_grad: bfloat16 [8, 4096, 1536], P('expert', None, 'dp')
- up_grad: bfloat16 [8, 4096, 1536], P('expert', None, 'dp')
- down_grad: bfloat16 [8, 1536, 4096], P('expert', 'dp')
The draws below stay inside these ranges and needn't reach their ends.
Inputs may be any that keep to these rules, and one draw needn't show every extreme that they name: `expert_ids`: each row names 8 different experts. Within the rows of one device no expert is named by more than 9 rows, a bound that some block reaches of them.
All inputs are finite; a program needn't handle non-finite values.
Results may differ from the reference program's by a relative error of at most 0.014.
Values may be sent and summed in bfloat16 or wider, within the bound.
A program may use at most 192 MiB of HBM per device.

```python
import math
import jax
import jax.numpy as jnp
import numpy as np
from jax import lax

D = 4096
FF = 1536
ALL_EXPERTS = 128
TOPK = 8
TOK_DEV = 128
EXPERTS = 8
CAP = 9
TOKENS = 4096
N_DP = 4
N_EXPERT = 8


def block_scale(own_key, shape, pieces, smallest, high):
    level, own = 1.0, jax.random.fold_in(own_key, 6)
    for position, shards_of in pieces:
        steps = jnp.exp(jax.random.uniform(jax.random.fold_in(own, position), (shards_of,), jnp.float32, smallest / len(pieces), high / len(pieces)))
        level = level * jnp.repeat(steps, shape[position] // shards_of).reshape([-1 if axis == position else 1 for axis in range(len(shape))])
    return level


def shared_out(key, own, number, rows, amount, top, limit, slope):
    ranking = jax.random.permutation(key, amount)
    heavy_load, ordinary = load_shares(amount, rows * top, limit, slope, True), load_shares(amount, rows * top, limit, slope, False)
    places = jnp.arange(amount)

    def named(sizes, offset_by):
        used = int((sizes > 0).sum())
        fixed = max(1, used // 4)
        passed = fixed + (places - fixed + offset_by * (used - fixed)) % max(1, amount - fixed)
        return jnp.zeros((amount,), jnp.int32).at[ranking[jnp.where(places < fixed, places, passed)]].set(jnp.asarray(sizes, jnp.int32))

    sizes = jnp.where(number % 4 == 0, named(heavy_load, number // 4), named(ordinary, number - number // 4 - 1))
    mixed = jax.random.permutation(jax.random.fold_in(own, 3), amount)
    source_of, taker = mixed[0:amount // 2 * 2:2], mixed[1:amount // 2 * 2:2]
    room = jnp.minimum(sizes[source_of] - 1, limit - sizes[taker]) // 2
    room = jnp.where((source_of == ranking[0]) | (taker == ranking[0]) | (sizes[taker] == 0), 0, jnp.maximum(room, 0))
    passed = jax.random.randint(jax.random.fold_in(own, 4), (amount // 2,), 0, 1 << 20) % (room + 1)
    sizes = sizes.at[source_of].add(-passed).at[taker].add(passed)
    labels = jnp.searchsorted(jnp.cumsum(sizes), jnp.arange(rows * top), side="right").astype(jnp.int32)
    listing = labels.reshape(top, rows).T
    listing = listing[jax.random.permutation(jax.random.fold_in(own, 1), rows)]
    offset_by = jax.random.randint(jax.random.fold_in(own, 2), (rows, 1), 0, top)
    return jnp.take_along_axis(listing, (jnp.arange(top)[None, :] + offset_by) % top, axis=1)


def load_shares(number_of, total, most, skew, full):
    weights = [(1 << 20) // math.isqrt(standing ** skew) + 1 for standing in range(1, number_of + 1)]
    largest = most if full else min(most, max(-(-total // number_of), total * weights[0] // sum(weights)))
    least = 1 if total - largest >= number_of - 1 else 0
    given, rest = [largest] + [least] * (number_of - 1), total - largest - least * (number_of - 1)
    while rest > 0:
        free = [i for i in range(1, number_of) if given[i] < largest] or [i for i in range(1, number_of) if given[i] < most]
        whole, remaining = sum([weights[i] for i in free]), rest
        for i in free:
            extra = min(most - given[i], max(1, remaining * weights[i] // whole), rest)
            given[i] = given[i] + extra
            rest = rest - extra
    return np.array(given)


def noise(key, dims, width, most, pieces=(), kind=jnp.bfloat16):
    gain = block_scale(key, dims, pieces, -0.22, 0.18) if pieces else 1.0
    values = jax.random.normal(key, dims, jnp.float32) * width * gain
    return jnp.minimum(jnp.maximum(values, -most), most).astype(kind)


def setup_inputs(seed: int = 0) -> dict:
    seeds = jax.random.split(jax.random.key(seed), 8)
    tokens = noise(seeds[0], (TOKENS, D), 1.0, 6.0, ((0, 32),))
    out_grad = noise(seeds[1], (TOKENS, D), 1.0, 6.0, ((0, 32),))
    expert_ids_keys = jax.random.split(jax.random.fold_in(seeds[2], 1), TOKENS // TOK_DEV)
    expert_ids_turns = jax.random.permutation(jax.random.fold_in(seeds[2], 3), TOKENS // TOK_DEV)
    expert_ids = jax.vmap(lambda own, number: shared_out(jax.random.fold_in(seeds[2], 2), own, number, TOK_DEV, ALL_EXPERTS, TOPK, CAP, 1))(expert_ids_keys, expert_ids_turns).reshape((TOKENS, TOPK))
    gate_weights = jnp.clip(jnp.exp(math.log(1.0) - 2.3025851 * jax.random.uniform(seeds[3], (TOKENS, TOPK), jnp.float32) ** block_scale(seeds[3], (TOKENS, TOPK), ((0, 32),), -0.2, 0.2)), 0.1, 1.0)
    w_gate = noise(seeds[4], (EXPERTS, D, FF), D ** -0.5, 0.09375, ((0, 8), (2, 4)))
    w_up = noise(seeds[5], (EXPERTS, D, FF), D ** -0.5, 0.09375, ((0, 8), (2, 4)))
    w_down = noise(seeds[6], (EXPERTS, FF, D), FF ** -0.5, 0.15625, ((0, 8), (1, 4)))
    return dict(tokens=tokens, out_grad=out_grad, expert_ids=expert_ids, gate_weights=gate_weights, w_gate=w_gate, w_up=w_up, w_down=w_down)


def slot_tables(expert_ids, gate_weights, experts, cap):
    tok_rows, choose = expert_ids.shape
    flat = expert_ids.reshape(-1).astype(jnp.int32)
    onehot = (flat[:, None] == jnp.arange(experts, dtype=jnp.int32)[None, :]).astype(jnp.int32)
    before = jnp.cumsum(onehot, axis=0) - onehot
    ranked = jnp.sum(before * onehot, axis=1).astype(jnp.int32)
    target = jnp.where(flat < experts, flat * cap + ranked, -1).reshape(tok_rows, choose)
    slots = jnp.arange(experts * cap, dtype=jnp.int32)
    hits = slots[:, None, None] == target[None, :, :]
    place = jnp.sum(hits.astype(jnp.float32), axis=2)
    scaled = jnp.sum(jnp.where(hits, gate_weights[None, :, :], jnp.float32(0.0)), axis=2)
    return place, scaled


def reference(tokens, out_grad, expert_ids, gate_weights, w_gate, w_up, w_down):
    blocks = N_DP * N_EXPERT
    experts = N_EXPERT
    group = FF // N_DP
    tok_b = tokens.reshape(blocks, TOK_DEV, D)
    dy_b = out_grad.reshape(blocks, TOK_DEV, D)
    ids_b = expert_ids.reshape(blocks, TOK_DEV, TOPK)
    gw_b = gate_weights.reshape(blocks, TOK_DEV, TOPK)
    place, scaled = jax.vmap(lambda a, b: slot_tables(a, b, experts, CAP))(ids_b, gw_b)

    def send(items):
        pl, sc, xb, db = items
        xs = jnp.dot(pl.astype(jnp.bfloat16), xb, preferred_element_type=jnp.float32).astype(jnp.bfloat16)
        ds = jnp.dot(sc, db.astype(jnp.float32), precision=lax.Precision.HIGHEST).astype(jnp.bfloat16)
        return xs, ds

    slot_x, slot_dy = lax.map(send, (place, scaled, tok_b, dy_b))
    slot_x = slot_x.reshape(blocks, experts, CAP, D).transpose(1, 0, 2, 3).reshape(experts, blocks * CAP, D)
    slot_dy = slot_dy.reshape(blocks, experts, CAP, D).transpose(1, 0, 2, 3).reshape(experts, blocks * CAP, D)

    def expert(items):
        xs, ds, wg, wu, wd = items
        gate = jnp.dot(xs, wg, preferred_element_type=jnp.float32)
        up = jnp.dot(xs, wu, preferred_element_type=jnp.float32)
        sig = jax.nn.sigmoid(gate)
        act = (gate * sig * up).astype(jnp.bfloat16)
        d_act = jnp.dot(ds, wd.T, preferred_element_type=jnp.float32)
        d_up = (d_act * gate * sig).astype(jnp.bfloat16)
        d_gate = (d_act * up * sig * (1.0 + gate * (1.0 - sig))).astype(jnp.bfloat16)
        g_gate = jnp.dot(xs.T, d_gate, preferred_element_type=jnp.float32).astype(jnp.bfloat16)
        g_up = jnp.dot(xs.T, d_up, preferred_element_type=jnp.float32).astype(jnp.bfloat16)
        g_down = jnp.dot(act.T, ds, preferred_element_type=jnp.float32).astype(jnp.bfloat16)
        rows = xs.shape[0]
        dg_s = d_gate.astype(jnp.float32).reshape(rows, N_DP, group)
        du_s = d_up.astype(jnp.float32).reshape(rows, N_DP, group)
        wg_s = wg.astype(jnp.float32).reshape(D, N_DP, group)
        wu_s = wu.astype(jnp.float32).reshape(D, N_DP, group)
        part = jnp.einsum("rpf,dpf->prd", dg_s, wg_s, precision=lax.Precision.HIGHEST)
        part = part + jnp.einsum("rpf,dpf->prd", du_s, wu_s, precision=lax.Precision.HIGHEST)
        part = part.astype(jnp.bfloat16).astype(jnp.float32)
        return g_gate, g_up, g_down, jnp.sum(part, axis=0).astype(jnp.bfloat16)

    gate_grad, up_grad, down_grad, combined = lax.map(expert, (slot_x, slot_dy, w_gate, w_up, w_down))
    combined = combined.reshape(experts, blocks, CAP, D).transpose(1, 0, 2, 3).reshape(blocks, experts * CAP, D)

    def gather_back(items):
        pl, cb = items
        return jnp.dot(pl.T.astype(jnp.bfloat16), cb, preferred_element_type=jnp.float32).astype(jnp.bfloat16)

    token_grad = lax.map(gather_back, (place, combined)).reshape(TOKENS, D)
    return token_grad, gate_grad, up_grad, down_grad
```

```python
import jax
import jax.numpy as jnp
from jax import lax
from jax.sharding import PartitionSpec as P

CAP = 9
MAIN = 8
DP = 4
OVER_ROWS = (((0,), (0,)), ((), ()))
OVER_UNITS = (((1,), (1,)), ((), ()))


def slot_tables(expert_ids, gate_weights, experts):
    tok_rows, choose = expert_ids.shape
    flat = expert_ids.reshape(-1)
    onehot = (flat[:, None] == jnp.arange(experts, dtype=jnp.int32)[None, :]).astype(jnp.int32)
    before = jnp.cumsum(onehot, axis=0) - onehot
    ranked = jnp.sum(before * onehot, axis=1)
    row = jnp.where(ranked < MAIN, flat * MAIN + ranked, experts * MAIN + flat)
    target = jnp.where(flat < experts, row, -1).reshape(tok_rows, choose)
    slots = jnp.arange(experts * CAP, dtype=jnp.int32)
    hits = slots[:, None, None] == target[None, :, :]
    place = jnp.sum(hits.astype(jnp.float32), axis=2)
    scaled = jnp.sum(jnp.where(hits, gate_weights[None, :, :], jnp.float32(0.0)), axis=2)
    return (place, scaled)


def pack(rows):
    blocks = rows.shape[0] // CAP
    width = rows.shape[1]
    main = rows[: blocks * MAIN]
    extra = rows[blocks * MAIN :].reshape(blocks * MAIN, width // MAIN)
    return jnp.concatenate([main, extra], axis=1)


def unpack(packed, width):
    main = packed[:, :width]
    extra = packed[:, width:].reshape(packed.shape[0] // MAIN, width)
    return jnp.concatenate([main, extra], axis=0)


def swap(value, bit):
    return lax.ppermute(value, "dp", [(i, i ^ bit) for i in range(DP)])


def gather(own):
    half = own.shape[1] // 2
    one = swap(own, 1)
    two = swap(own, 2)
    three_a = swap(one[:, :half], 2)
    three_b = swap(two[:, half:], 1)
    return jnp.concatenate([own, one, two, jnp.concatenate([three_a, three_b], axis=1)], axis=0)


def reduce_to_own(parts):
    rows = parts.shape[0] // DP
    half = parts.shape[1] // 2
    f32 = jnp.float32
    p = [parts[r * rows : (r + 1) * rows] for r in range(DP)]

    def way(cols, first, second):
        got = swap(jnp.concatenate([p[first][:, cols], p[3][:, cols]], axis=0), first)
        onward = p[second][:, cols].astype(f32) + got[rows:].astype(f32)
        last = swap(onward.astype(jnp.bfloat16), second)
        return p[0][:, cols].astype(f32) + got[:rows].astype(f32) + last.astype(f32)

    a = way(slice(0, half), 1, 2)
    b = way(slice(half, 2 * half), 2, 1)
    return jnp.concatenate([a, b], axis=1).astype(jnp.bfloat16)


def exchange(packed, experts):
    blocks = packed.reshape(experts, MAIN, -1)
    got = lax.all_to_all(blocks, "expert", split_axis=0, concat_axis=0, tiled=True)
    return got.reshape(packed.shape)


def shards(tokens, out_grad, expert_ids, gate_weights, w_gate, w_up, w_down):
    experts = lax.axis_size("expert")
    width = tokens.shape[1]
    bf16, f32 = jnp.bfloat16, jnp.float32
    place, scaled = slot_tables(expert_ids, gate_weights, experts)
    place_bf = place.astype(bf16)
    send_x = jnp.dot(place_bf, tokens, preferred_element_type=f32).astype(bf16)
    send_dy = jnp.dot(scaled, out_grad.astype(f32), precision=lax.Precision.HIGHEST).astype(bf16)
    slot_x = unpack(gather(exchange(pack(send_x), experts)), width)
    slot_dy = unpack(gather(exchange(pack(send_dy), experts)), width)
    wg = w_gate[0]
    wu = w_up[0]
    wd = w_down[0]
    gate = jnp.dot(slot_x, wg, preferred_element_type=f32)
    up = jnp.dot(slot_x, wu, preferred_element_type=f32)
    sig = jax.nn.sigmoid(gate)
    act = (gate * sig * up).astype(bf16)
    d_act = lax.dot_general(slot_dy, wd, OVER_UNITS, preferred_element_type=f32)
    d_up = (d_act * gate * sig).astype(bf16)
    d_gate = (d_act * up * sig * (1.0 + gate * (1.0 - sig))).astype(bf16)
    partial = lax.dot_general(d_gate, wg, OVER_UNITS, preferred_element_type=f32)
    partial = partial + lax.dot_general(d_up, wu, OVER_UNITS, preferred_element_type=f32)
    slot_grad = reduce_to_own(pack(partial.astype(bf16)))
    gate_grad = lax.dot_general(slot_x, d_gate, OVER_ROWS, preferred_element_type=f32).astype(bf16)
    up_grad = lax.dot_general(slot_x, d_up, OVER_ROWS, preferred_element_type=f32).astype(bf16)
    down_grad = lax.dot_general(act, slot_dy, OVER_ROWS, preferred_element_type=f32).astype(bf16)
    returned = unpack(exchange(slot_grad, experts), width)
    token_grad = lax.dot_general(place_bf, returned, OVER_ROWS, preferred_element_type=f32)
    return (token_grad.astype(bf16), gate_grad[None], up_grad[None], down_grad[None])


def solution(mesh):
    return jax.shard_map(
        shards,
        mesh=mesh,
        in_specs=(
            P(("dp", "expert"), None),
            P(("dp", "expert"), None),
            P(("dp", "expert"), None),
            P(("dp", "expert"), None),
            P("expert", None, "dp"),
            P("expert", None, "dp"),
            P("expert", "dp", None),
        ),
        out_specs=(
            P(("dp", "expert"), None),
            P("expert", None, "dp"),
            P("expert", None, "dp"),
            P("expert", "dp", None),
        ),
        check_vma=False,
    )
```

```python
import functools

import jax
import jax.numpy as jnp
from jax import lax
from jax.experimental import pallas as pl
from jax.experimental.pallas import tpu as pltpu
from jax.sharding import PartitionSpec as P

CAP = 9
MAIN = 8
DP = 4
OVER_ROWS = (((0,), (0,)), ((), ()))
OVER_UNITS = (((1,), (1,)), ((), ()))


def slot_tables(expert_ids, gate_weights, experts):
    tok_rows, choose = expert_ids.shape
    flat = expert_ids.reshape(-1)
    onehot = (flat[:, None] == jnp.arange(experts, dtype=jnp.int32)[None, :]).astype(jnp.int32)
    before = jnp.cumsum(onehot, axis=0) - onehot
    ranked = jnp.sum(before * onehot, axis=1)
    row = jnp.where(ranked < MAIN, flat * MAIN + ranked, experts * MAIN + flat)
    target = jnp.where(flat < experts, row, -1).reshape(tok_rows, choose)
    slots = jnp.arange(experts * CAP, dtype=jnp.int32)
    hits = slots[:, None, None] == target[None, :, :]
    place = jnp.sum(hits.astype(jnp.float32), axis=2)
    scaled = jnp.sum(jnp.where(hits, gate_weights[None, :, :], jnp.float32(0.0)), axis=2)
    return (place, scaled)


def pack(rows):
    blocks = rows.shape[0] // CAP
    width = rows.shape[1]
    main = rows[: blocks * MAIN]
    extra = rows[blocks * MAIN :].reshape(blocks * MAIN, width // MAIN)
    return jnp.concatenate([main, extra], axis=1)


def unpack(packed, width):
    main = packed[:, :width]
    extra = packed[:, width:].reshape(packed.shape[0] // MAIN, width)
    return jnp.concatenate([main, extra], axis=0)


def swap(value, bit):
    return lax.ppermute(value, "dp", [(i, i ^ bit) for i in range(DP)])


def visit_order(experts):
    order = [0]
    for k in range(1, experts // 2 + 1):
        order.append(k)
        if experts - k != k:
            order.append(experts - k)
    return order


def enter(me, pe, experts, neighbours):
    barrier = pltpu.get_barrier_semaphore()
    for k in range(1, experts):
        pl.semaphore_signal(
            barrier,
            inc=1,
            device_id=(me, lax.rem(pe + k, experts)),
            device_id_type=pl.DeviceIdType.MESH,
        )
    for other in neighbours:
        pl.semaphore_signal(
            barrier, inc=1, device_id=(other, pe), device_id_type=pl.DeviceIdType.MESH
        )
    pl.semaphore_wait(barrier, experts - 1 + len(neighbours))


def remote(src, dst, sems, slot, device):
    return pltpu.make_async_remote_copy(
        src_ref=src,
        dst_ref=dst,
        send_sem=sems.at[0, slot],
        recv_sem=sems.at[1, slot],
        device_id=device,
        device_id_type=pl.DeviceIdType.MESH,
    )


def dispatch_kernel(experts, send, got, own_sem, z_sem, x_sem, y_sem, xy_sem, yx_sem):
    me, pe = lax.axis_index("dp"), lax.axis_index("expert")
    along_x = me + 1 - 2 * lax.rem(me, 2)
    along_y = lax.rem(me + 2, DP)
    half = send.shape[2] // 2
    first, last = pl.ds(0, half), pl.ds(half, half)
    enter(me, pe, experts, (along_x, along_y))
    own = pltpu.make_async_copy(send.at[pe], got.at[0, pe], own_sem)
    own.start()
    order = visit_order(experts)
    across = {}
    for k in order[1:]:
        to = lax.rem(pe + k, experts)
        across[k] = remote(send.at[to], got.at[0, pe], z_sem, k, (me, to))
        across[k].start()
    copies = {}
    for step in range(experts + 1):
        if step < experts:
            k = order[step]
            block = lax.rem(pe + experts - k, experts)
            if k == 0:
                source = send.at[pe]
            else:
                across[k].wait_recv()
                source = got.at[0, block]
            ways = (
                remote(source, got.at[1, block], x_sem, k, (along_x, pe)),
                remote(source, got.at[2, block], y_sem, k, (along_y, pe)),
            )
            for way in ways:
                way.start()
            copies[k] = list(ways)
        if step >= 1:
            k = order[step - 1]
            block = lax.rem(pe + experts - k, experts)
            copies[k][0].wait_recv()
            onward = remote(
                got.at[1, block, :, first], got.at[3, block, :, first], xy_sem, k, (along_y, pe)
            )
            onward.start()
            copies[k].append(onward)
            copies[k][1].wait_recv()
            onward = remote(
                got.at[2, block, :, last], got.at[3, block, :, last], yx_sem, k, (along_x, pe)
            )
            onward.start()
            copies[k].append(onward)
    own.wait()
    for k in order:
        if k != 0:
            across[k].wait_send()
        for copy in copies[k]:
            copy.wait_send()
        copies[k][2].wait_recv()
        copies[k][3].wait_recv()


def dispatch(send):
    experts = send.shape[0]
    pairs = pltpu.SemaphoreType.DMA((2, experts))
    size = send.size * send.dtype.itemsize
    return pl.pallas_call(
        functools.partial(dispatch_kernel, experts),
        out_shape=jax.ShapeDtypeStruct((DP,) + send.shape, send.dtype),
        in_specs=[pl.BlockSpec(memory_space=pl.ANY)],
        out_specs=pl.BlockSpec(memory_space=pl.ANY),
        scratch_shapes=[pltpu.SemaphoreType.DMA(())] + [pairs] * 5,
        compiler_params=pltpu.CompilerParams(collective_id=0, has_side_effects=True),
        cost_estimate=pl.CostEstimate(flops=0, bytes_accessed=8 * size, transcendentals=0),
    )(send)


def exchange_kernel(experts, send, got, own_sem, z_sem):
    me, pe = lax.axis_index("dp"), lax.axis_index("expert")
    enter(me, pe, experts, ())
    own = pltpu.make_async_copy(send.at[pe], got.at[pe], own_sem)
    own.start()
    across = []
    for k in visit_order(experts)[1:]:
        to = lax.rem(pe + k, experts)
        across.append(remote(send.at[to], got.at[pe], z_sem, k, (me, to)))
        across[-1].start()
    own.wait()
    for copy in across:
        copy.wait()


def exchange(send):
    experts = send.shape[0]
    size = send.size * send.dtype.itemsize
    return pl.pallas_call(
        functools.partial(exchange_kernel, experts),
        out_shape=jax.ShapeDtypeStruct(send.shape, send.dtype),
        in_specs=[pl.BlockSpec(memory_space=pl.ANY)],
        out_specs=pl.BlockSpec(memory_space=pl.ANY),
        scratch_shapes=[pltpu.SemaphoreType.DMA(()), pltpu.SemaphoreType.DMA((2, experts))],
        compiler_params=pltpu.CompilerParams(collective_id=1, has_side_effects=True),
        cost_estimate=pl.CostEstimate(flops=0, bytes_accessed=4 * size, transcendentals=0),
    )(send)


def reduce_to_own(parts):
    rows = parts.shape[0] // DP
    half = parts.shape[1] // 2
    f32 = jnp.float32
    p = [parts[r * rows : (r + 1) * rows] for r in range(DP)]

    def way(cols, first, second):
        got = swap(jnp.concatenate([p[first][:, cols], p[3][:, cols]], axis=0), first)
        onward = p[second][:, cols].astype(f32) + got[rows:].astype(f32)
        last = swap(onward.astype(jnp.bfloat16), second)
        return p[0][:, cols].astype(f32) + got[:rows].astype(f32) + last.astype(f32)

    a = way(slice(0, half), 1, 2)
    b = way(slice(half, 2 * half), 2, 1)
    return jnp.concatenate([a, b], axis=1).astype(jnp.bfloat16)


def shards(tokens, out_grad, expert_ids, gate_weights, w_gate, w_up, w_down):
    experts = lax.axis_size("expert")
    width = tokens.shape[1]
    bf16, f32 = jnp.bfloat16, jnp.float32
    place, scaled = slot_tables(expert_ids, gate_weights, experts)
    place_bf = place.astype(bf16)
    send_x = jnp.dot(place_bf, tokens, preferred_element_type=f32).astype(bf16)
    send_dy = jnp.dot(scaled, out_grad.astype(f32), precision=lax.Precision.HIGHEST).astype(bf16)
    both = [pack(rows).reshape(experts, MAIN, -1) for rows in (send_x, send_dy)]
    got = dispatch(jnp.concatenate(both, axis=1))
    slot_x = unpack(got[:, :, :MAIN].reshape(DP * experts * MAIN, -1), width)
    slot_dy = unpack(got[:, :, MAIN:].reshape(DP * experts * MAIN, -1), width)
    wg = w_gate[0]
    wu = w_up[0]
    wd = w_down[0]
    gate = jnp.dot(slot_x, wg, preferred_element_type=f32)
    up = jnp.dot(slot_x, wu, preferred_element_type=f32)
    sig = jax.nn.sigmoid(gate)
    act = (gate * sig * up).astype(bf16)
    d_act = lax.dot_general(slot_dy, wd, OVER_UNITS, preferred_element_type=f32)
    d_up = (d_act * gate * sig).astype(bf16)
    d_gate = (d_act * up * sig * (1.0 + gate * (1.0 - sig))).astype(bf16)
    partial = lax.dot_general(d_gate, wg, OVER_UNITS, preferred_element_type=f32)
    partial = partial + lax.dot_general(d_up, wu, OVER_UNITS, preferred_element_type=f32)
    slot_grad = reduce_to_own(pack(partial.astype(bf16)))
    gate_grad = lax.dot_general(slot_x, d_gate, OVER_ROWS, preferred_element_type=f32).astype(bf16)
    up_grad = lax.dot_general(slot_x, d_up, OVER_ROWS, preferred_element_type=f32).astype(bf16)
    down_grad = lax.dot_general(act, slot_dy, OVER_ROWS, preferred_element_type=f32).astype(bf16)
    slot_grad, gate_grad, up_grad, down_grad = lax.optimization_barrier(
        (slot_grad, gate_grad, up_grad, down_grad)
    )
    blocks = slot_grad.reshape(experts, MAIN, -1)
    half = blocks.shape[2] // 2
    back = exchange(jnp.concatenate([blocks[:, :, :half], blocks[:, :, half:]], axis=1))
    back = jnp.concatenate([back[:, :MAIN], back[:, MAIN:]], axis=2)
    returned = unpack(back.reshape(experts * MAIN, -1), width)
    token_grad = lax.dot_general(place_bf, returned, OVER_ROWS, preferred_element_type=f32)
    return (token_grad.astype(bf16), gate_grad[None], up_grad[None], down_grad[None])


def solution(mesh):
    return jax.shard_map(
        shards,
        mesh=mesh,
        in_specs=(
            P(("dp", "expert"), None),
            P(("dp", "expert"), None),
            P(("dp", "expert"), None),
            P(("dp", "expert"), None),
            P("expert", None, "dp"),
            P("expert", None, "dp"),
            P("expert", "dp", None),
        ),
        out_specs=(
            P(("dp", "expert"), None),
            P("expert", None, "dp"),
            P("expert", None, "dp"),
            P("expert", "dp", None),
        ),
        check_vma=False,
    )
```

```python
import functools

import jax
import jax.numpy as jnp
from jax import lax
from jax.experimental import pallas as pl
from jax.experimental.pallas import tpu as pltpu
from jax.sharding import PartitionSpec as P

CAP = 9
MAIN = 8
DP = 4
OVER_ROWS = (((0,), (0,)), ((), ()))
OVER_UNITS = (((1,), (1,)), ((), ()))


def slot_tables(expert_ids, gate_weights, experts):
    tok_rows, choose = expert_ids.shape
    flat = expert_ids.reshape(-1)
    onehot = (flat[:, None] == jnp.arange(experts, dtype=jnp.int32)[None, :]).astype(jnp.int32)
    before = jnp.cumsum(onehot, axis=0) - onehot
    ranked = jnp.sum(before * onehot, axis=1)
    row = jnp.where(ranked < MAIN, flat * MAIN + ranked, experts * MAIN + flat)
    target = jnp.where(flat < experts, row, -1).reshape(tok_rows, choose)
    slots = jnp.arange(experts * CAP, dtype=jnp.int32)
    hits = slots[:, None, None] == target[None, :, :]
    place = jnp.sum(hits.astype(jnp.float32), axis=2)
    scaled = jnp.sum(jnp.where(hits, gate_weights[None, :, :], jnp.float32(0.0)), axis=2)
    return (place, scaled)


def one_hot(shape, column_of_row, dim=0):
    along = lax.broadcasted_iota(jnp.int32, shape, dim)
    across = lax.broadcasted_iota(jnp.int32, shape, 1 - dim)
    return (column_of_row(along) == across).astype(jnp.bfloat16)


def expert_kernel(
    z, z_extra, wg, wu, wd, x, dy, act, d_gate, d_up, partial, gate_sum, up_sum, act_sum, extra_sum
):
    f32, bf16 = jnp.float32, jnp.bfloat16
    step = pl.program_id(0)
    rows2 = z.shape[0]
    main = rows2 // 2
    blocks = main // MAIN

    def dot(a, b, dims=(((1,), (0,)), ((), ()))):
        return lax.dot_general(a, b, dims, preferred_element_type=f32)

    @pl.when(step == 0)
    def _():
        for total in (gate_sum, up_sum, act_sum):
            total[...] = jnp.zeros_like(total)

    @pl.when(step < MAIN)
    def _():
        for out, offset in ((x, 0), (dy, MAIN)):
            pick = one_hot((main, rows2), lambda r: (r // MAIN) * 2 * MAIN + r % MAIN + offset)
            out[:main, :] = dot(pick, z[...]).astype(bf16)
            pick = one_hot((blocks, rows2), lambda r: r * 2 * MAIN + offset + step)
            out[main:, :] = dot(pick, z_extra[...]).astype(bf16)
        gate_sum[...] += dot(x[...], wg[...])
        up_sum[...] += dot(x[...], wu[...])
        act_sum[...] += dot(dy[...], wd[...], OVER_UNITS)

    @pl.when(step == MAIN - 1)
    def _():
        gate, up, d_act = gate_sum[...], up_sum[...], act_sum[...]
        sig = jax.nn.sigmoid(gate)
        act[...] = (gate * sig * up).astype(bf16)
        d_up[...] = (d_act * gate * sig).astype(bf16)
        d_gate[...] = (d_act * up * sig * (1.0 + gate * (1.0 - sig))).astype(bf16)
        extra_sum[...] = jnp.zeros_like(extra_sum)

    @pl.when((step >= MAIN) & (step < 2 * MAIN))
    def _():
        value = dot(d_gate[...], wg[...], OVER_UNITS) + dot(d_up[...], wu[...], OVER_UNITS)
        value = value.astype(bf16)
        partial[...] = value[:main]
        put = one_hot((main, blocks), lambda r: r * MAIN + (step - MAIN), 1)
        extra_sum[...] += dot(put, value[main:])

    @pl.when(step == 2 * MAIN)
    def _():
        partial[...] = extra_sum[...].astype(bf16)


def expert_block(z, wg, wu, wd):
    f32, bf16 = jnp.float32, jnp.bfloat16
    rows2, packed = z.shape
    width, units = wg.shape
    piece = width // MAIN
    main = rows2 // 2
    rows = main // MAIN * CAP

    def forth(i):
        return jnp.minimum(i, MAIN - 1)

    def both(i):
        return jnp.where(i < MAIN, i, jnp.minimum(i - MAIN, MAIN - 1))

    def after(i):
        return jnp.maximum(i - MAIN, 0)

    wide = pl.BlockSpec((rows, piece), lambda i: (0, forth(i)))
    whole = pl.BlockSpec((rows, units), lambda i: (0, 0))
    sums = pltpu.VMEM((rows, units), f32)
    hidden = jax.ShapeDtypeStruct((rows, units), bf16)
    tall = jax.ShapeDtypeStruct((rows, width), bf16)
    return pl.pallas_call(
        expert_kernel,
        grid=(2 * MAIN + 1,),
        in_specs=[
            pl.BlockSpec((rows2, piece), lambda i: (0, forth(i))),
            pl.BlockSpec((rows2, piece), lambda i: (0, MAIN)),
            pl.BlockSpec((piece, units), lambda i: (both(i), 0)),
            pl.BlockSpec((piece, units), lambda i: (both(i), 0)),
            pl.BlockSpec((units, piece), lambda i: (0, forth(i))),
        ],
        out_specs=[wide, wide, whole, whole, whole]
        + [pl.BlockSpec((main, piece), lambda i: (0, after(i)))],
        out_shape=[tall, tall, hidden, hidden, hidden]
        + [jax.ShapeDtypeStruct((main, packed), bf16)],
        scratch_shapes=[sums, sums, sums, pltpu.VMEM((main, piece), f32)],
        compiler_params=pltpu.CompilerParams(vmem_limit_bytes=48 * 1024 * 1024),
        cost_estimate=pl.CostEstimate(
            flops=10 * rows * width * units,
            bytes_accessed=10 * width * units + 12 * rows * width,
            transcendentals=rows * units,
        ),
    )(z, z, wg, wu, wd)


def pack(rows):
    blocks = rows.shape[0] // CAP
    width = rows.shape[1]
    main = rows[: blocks * MAIN]
    extra = rows[blocks * MAIN :].reshape(blocks * MAIN, width // MAIN)
    return jnp.concatenate([main, extra], axis=1)


def unpack(packed, width):
    main = packed[:, :width]
    extra = packed[:, width:].reshape(packed.shape[0] // MAIN, width)
    return jnp.concatenate([main, extra], axis=0)


def swap(value, bit):
    return lax.ppermute(value, "dp", [(i, i ^ bit) for i in range(DP)])


def visit_order(experts):
    order = [0]
    for k in range(1, experts // 2 + 1):
        order.append(k)
        if experts - k != k:
            order.append(experts - k)
    return order


def enter(me, pe, experts, neighbours):
    barrier = pltpu.get_barrier_semaphore()
    for k in range(1, experts):
        pl.semaphore_signal(
            barrier,
            inc=1,
            device_id=(me, lax.rem(pe + k, experts)),
            device_id_type=pl.DeviceIdType.MESH,
        )
    for other in neighbours:
        pl.semaphore_signal(
            barrier, inc=1, device_id=(other, pe), device_id_type=pl.DeviceIdType.MESH
        )
    pl.semaphore_wait(barrier, experts - 1 + len(neighbours))


def remote(src, dst, sems, slot, device):
    return pltpu.make_async_remote_copy(
        src_ref=src,
        dst_ref=dst,
        send_sem=sems.at[0, slot],
        recv_sem=sems.at[1, slot],
        device_id=device,
        device_id_type=pl.DeviceIdType.MESH,
    )


def dispatch_kernel(experts, send, got, own_sem, z_sem, x_sem, y_sem, xy_sem, yx_sem):
    me, pe = lax.axis_index("dp"), lax.axis_index("expert")
    along_x = me + 1 - 2 * lax.rem(me, 2)
    along_y = lax.rem(me + 2, DP)
    half = send.shape[2] // 2
    first, last = pl.ds(0, half), pl.ds(half, half)
    side_size = experts // 2
    side, low = lax.div(pe, side_size), lax.rem(pe, side_size)

    def other(cross, turn):
        base = (1 - side if cross else side) * side_size
        return base + lax.rem(low + turn, side_size)

    near = [(0, q) for q in range(1, side_size)]
    far = [(1, q) for q in range(side_size)]
    order = [(0, 0)]
    for i in range(side_size):
        order += near[i : i + 1] + far[i : i + 1]
    enter(me, pe, experts, (along_x, along_y))
    own = pltpu.make_async_copy(send.at[pe], got.at[0, pe], own_sem)
    across, sent = {}, []
    for c, q in near + far:
        to = other(c, q)
        across[c, q] = remote(send.at[to], got.at[0, pe], z_sem, c * side_size + q, (me, to))
    at_once = 2
    for item in far[:at_once] + near:
        across[item].start()
    waiting = far[at_once:]
    copies = {}
    for step in range(experts + 1):
        if step < experts:
            c, q = item = order[step]
            slot = c * side_size + q
            block = other(c, side_size - q)
            if step == 0:
                source = send.at[pe]
            else:
                across[item].wait_recv()
                source = got.at[0, block]
            ways = (
                remote(source, got.at[1, block], x_sem, slot, (along_x, pe)),
                remote(source, got.at[2, block], y_sem, slot, (along_y, pe)),
            )
            for way in ways:
                way.start()
            copies[item] = list(ways)
            if step == 0:
                own.start()
            if c == 1 and waiting:
                across[item].wait_send()
                sent.append(item)
                across[waiting.pop(0)].start()
        if step >= 1:
            c, q = item = order[step - 1]
            slot = c * side_size + q
            block = other(c, side_size - q)
            copies[item][0].wait_recv()
            onward = remote(
                got.at[1, block, :, first], got.at[3, block, :, first], xy_sem, slot, (along_y, pe)
            )
            onward.start()
            copies[item].append(onward)
            copies[item][1].wait_recv()
            onward = remote(
                got.at[2, block, :, last], got.at[3, block, :, last], yx_sem, slot, (along_x, pe)
            )
            onward.start()
            copies[item].append(onward)
    own.wait()
    for item in order:
        if item != (0, 0) and item not in sent:
            across[item].wait_send()
        for copy in copies[item]:
            copy.wait_send()
        copies[item][2].wait_recv()
        copies[item][3].wait_recv()


def dispatch(send):
    experts = send.shape[0]
    pairs = pltpu.SemaphoreType.DMA((2, experts))
    size = send.size * send.dtype.itemsize
    return pl.pallas_call(
        functools.partial(dispatch_kernel, experts),
        out_shape=jax.ShapeDtypeStruct((DP,) + send.shape, send.dtype),
        in_specs=[pl.BlockSpec(memory_space=pl.ANY)],
        out_specs=pl.BlockSpec(memory_space=pl.ANY),
        scratch_shapes=[pltpu.SemaphoreType.DMA(())] + [pairs] * 5,
        compiler_params=pltpu.CompilerParams(collective_id=0, has_side_effects=True),
        cost_estimate=pl.CostEstimate(flops=0, bytes_accessed=8 * size, transcendentals=0),
    )(send)


def exchange_kernel(experts, send, got, own_sem, z_sem):
    me, pe = lax.axis_index("dp"), lax.axis_index("expert")
    enter(me, pe, experts, ())
    own = pltpu.make_async_copy(send.at[pe], got.at[pe], own_sem)
    own.start()
    across = []
    for k in visit_order(experts)[1:]:
        to = lax.rem(pe + k, experts)
        across.append(remote(send.at[to], got.at[pe], z_sem, k, (me, to)))
        across[-1].start()
    own.wait()
    for copy in across:
        copy.wait()


def exchange(send):
    experts = send.shape[0]
    size = send.size * send.dtype.itemsize
    return pl.pallas_call(
        functools.partial(exchange_kernel, experts),
        out_shape=jax.ShapeDtypeStruct(send.shape, send.dtype),
        in_specs=[pl.BlockSpec(memory_space=pl.ANY)],
        out_specs=pl.BlockSpec(memory_space=pl.ANY),
        scratch_shapes=[pltpu.SemaphoreType.DMA(()), pltpu.SemaphoreType.DMA((2, experts))],
        compiler_params=pltpu.CompilerParams(collective_id=1, has_side_effects=True),
        cost_estimate=pl.CostEstimate(flops=0, bytes_accessed=4 * size, transcendentals=0),
    )(send)


def reduce_to_own(parts):
    rows = parts.shape[0] // DP
    half = parts.shape[1] // 2
    f32 = jnp.float32
    p = [parts[r * rows : (r + 1) * rows] for r in range(DP)]

    def way(cols, first, second):
        got = swap(jnp.concatenate([p[first][:, cols], p[3][:, cols]], axis=0), first)
        onward = p[second][:, cols].astype(f32) + got[rows:].astype(f32)
        last = swap(onward.astype(jnp.bfloat16), second)
        return p[0][:, cols].astype(f32) + got[:rows].astype(f32) + last.astype(f32)

    a = way(slice(0, half), 1, 2)
    b = way(slice(half, 2 * half), 2, 1)
    return jnp.concatenate([a, b], axis=1).astype(jnp.bfloat16)


def shards(tokens, out_grad, expert_ids, gate_weights, w_gate, w_up, w_down):
    experts = lax.axis_size("expert")
    width = tokens.shape[1]
    bf16, f32 = jnp.bfloat16, jnp.float32
    place, scaled = slot_tables(expert_ids, gate_weights, experts)
    place_bf = place.astype(bf16)
    send_x = jnp.dot(place_bf, tokens, preferred_element_type=f32).astype(bf16)
    send_dy = jnp.dot(scaled, out_grad.astype(f32), precision=lax.Precision.HIGHEST).astype(bf16)
    both = [pack(rows).reshape(experts, MAIN, -1) for rows in (send_x, send_dy)]
    got = dispatch(jnp.concatenate(both, axis=1))
    z = got.reshape(DP * experts * 2 * MAIN, -1)
    slot_x, slot_dy, act, d_gate, d_up, partial = expert_block(z, w_gate[0], w_up[0], w_down[0])
    slot_grad = reduce_to_own(partial)
    gate_grad = lax.dot_general(slot_x, d_gate, OVER_ROWS, preferred_element_type=f32).astype(bf16)
    up_grad = lax.dot_general(slot_x, d_up, OVER_ROWS, preferred_element_type=f32).astype(bf16)
    down_grad = lax.dot_general(act, slot_dy, OVER_ROWS, preferred_element_type=f32).astype(bf16)
    slot_grad, gate_grad, up_grad, down_grad = lax.optimization_barrier(
        (slot_grad, gate_grad, up_grad, down_grad)
    )
    blocks = slot_grad.reshape(experts, MAIN, -1)
    half = blocks.shape[2] // 2
    back = exchange(jnp.concatenate([blocks[:, :, :half], blocks[:, :, half:]], axis=1))
    back = jnp.concatenate([back[:, :MAIN], back[:, MAIN:]], axis=2)
    returned = unpack(back.reshape(experts * MAIN, -1), width)
    token_grad = lax.dot_general(place_bf, returned, OVER_ROWS, preferred_element_type=f32)
    return (token_grad.astype(bf16), gate_grad[None], up_grad[None], down_grad[None])


def solution(mesh):
    return jax.shard_map(
        shards,
        mesh=mesh,
        in_specs=(
            P(("dp", "expert"), None),
            P(("dp", "expert"), None),
            P(("dp", "expert"), None),
            P(("dp", "expert"), None),
            P("expert", None, "dp"),
            P("expert", None, "dp"),
            P("expert", "dp", None),
        ),
        out_specs=(
            P(("dp", "expert"), None),
            P("expert", None, "dp"),
            P("expert", None, "dp"),
            P("expert", "dp", None),
        ),
        check_vma=False,
    )
```

```python
import functools

import jax
import jax.numpy as jnp
from jax import lax
from jax.experimental import pallas as pl
from jax.experimental.pallas import tpu as pltpu
from jax.sharding import PartitionSpec as P

CAP = 9
MAIN = 8
DP = 4
OVER_ROWS = (((0,), (0,)), ((), ()))
OVER_UNITS = (((1,), (1,)), ((), ()))


def slot_tables(expert_ids, gate_weights, experts):
    tok_rows, choose = expert_ids.shape
    flat = expert_ids.reshape(-1)
    onehot = (flat[:, None] == jnp.arange(experts, dtype=jnp.int32)[None, :]).astype(jnp.int32)
    before = jnp.cumsum(onehot, axis=0) - onehot
    ranked = jnp.sum(before * onehot, axis=1)
    row = jnp.where(ranked < MAIN, flat * MAIN + ranked, experts * MAIN + flat)
    target = jnp.where(flat < experts, row, -1).reshape(tok_rows, choose)
    slots = jnp.arange(experts * CAP, dtype=jnp.int32)
    hits = slots[:, None, None] == target[None, :, :]
    place = jnp.sum(hits.astype(jnp.float32), axis=2)
    scaled = jnp.sum(jnp.where(hits, gate_weights[None, :, :], jnp.float32(0.0)), axis=2)
    return (place, scaled)


def one_hot(shape, column_of_row, dim=0):
    along = lax.broadcasted_iota(jnp.int32, shape, dim)
    across = lax.broadcasted_iota(jnp.int32, shape, 1 - dim)
    return (column_of_row(along) == across).astype(jnp.bfloat16)


def expert_kernel(
    z, z_extra, wg, wu, wd, x, dy, act, d_gate, d_up, partial, gate_sum, up_sum, act_sum, extra_sum
):
    f32, bf16 = jnp.float32, jnp.bfloat16
    step = pl.program_id(0)
    rows2 = z.shape[0]
    main = rows2 // 2
    blocks = main // MAIN

    def dot(a, b, dims=(((1,), (0,)), ((), ()))):
        return lax.dot_general(a, b, dims, preferred_element_type=f32)

    @pl.when(step == 0)
    def _():
        for total in (gate_sum, up_sum, act_sum):
            total[...] = jnp.zeros_like(total)

    @pl.when(step < MAIN)
    def _():
        for out, offset in ((x, 0), (dy, MAIN)):
            pick = one_hot((main, rows2), lambda r: (r // MAIN) * 2 * MAIN + r % MAIN + offset)
            out[:main, :] = dot(pick, z[...]).astype(bf16)
            pick = one_hot((blocks, rows2), lambda r: r * 2 * MAIN + offset + step)
            out[main:, :] = dot(pick, z_extra[...]).astype(bf16)
        gate_sum[...] += dot(x[...], wg[...])
        up_sum[...] += dot(x[...], wu[...])
        act_sum[...] += dot(dy[...], wd[...], OVER_UNITS)

    @pl.when(step == MAIN - 1)
    def _():
        gate, up, d_act = gate_sum[...], up_sum[...], act_sum[...]
        sig = jax.nn.sigmoid(gate)
        act[...] = (gate * sig * up).astype(bf16)
        d_up[...] = (d_act * gate * sig).astype(bf16)
        d_gate[...] = (d_act * up * sig * (1.0 + gate * (1.0 - sig))).astype(bf16)
        extra_sum[...] = jnp.zeros_like(extra_sum)

    @pl.when((step >= MAIN) & (step < 2 * MAIN))
    def _():
        value = dot(d_gate[...], wg[...], OVER_UNITS) + dot(d_up[...], wu[...], OVER_UNITS)
        value = value.astype(bf16)
        partial[...] = value[:main]
        put = one_hot((main, blocks), lambda r: r * MAIN + (step - MAIN), 1)
        extra_sum[...] += dot(put, value[main:])

    @pl.when(step == 2 * MAIN)
    def _():
        partial[...] = extra_sum[...].astype(bf16)


def expert_block(z, wg, wu, wd):
    f32, bf16 = jnp.float32, jnp.bfloat16
    rows2, packed = z.shape
    width, units = wg.shape
    piece = width // MAIN
    main = rows2 // 2
    rows = main // MAIN * CAP

    def forth(i):
        return jnp.minimum(i, MAIN - 1)

    def both(i):
        return jnp.where(i < MAIN, i, jnp.minimum(i - MAIN, MAIN - 1))

    def after(i):
        return jnp.maximum(i - MAIN, 0)

    wide = pl.BlockSpec((rows, piece), lambda i: (0, forth(i)))
    whole = pl.BlockSpec((rows, units), lambda i: (0, 0))
    sums = pltpu.VMEM((rows, units), f32)
    hidden = jax.ShapeDtypeStruct((rows, units), bf16)
    tall = jax.ShapeDtypeStruct((rows, width), bf16)
    return pl.pallas_call(
        expert_kernel,
        grid=(2 * MAIN + 1,),
        in_specs=[
            pl.BlockSpec((rows2, piece), lambda i: (0, forth(i))),
            pl.BlockSpec((rows2, piece), lambda i: (0, MAIN)),
            pl.BlockSpec((piece, units), lambda i: (both(i), 0)),
            pl.BlockSpec((piece, units), lambda i: (both(i), 0)),
            pl.BlockSpec((units, piece), lambda i: (0, forth(i))),
        ],
        out_specs=[wide, wide, whole, whole, whole]
        + [pl.BlockSpec((main, piece), lambda i: (0, after(i)))],
        out_shape=[tall, tall, hidden, hidden, hidden]
        + [jax.ShapeDtypeStruct((main, packed), bf16)],
        scratch_shapes=[sums, sums, sums, pltpu.VMEM((main, piece), f32)],
        compiler_params=pltpu.CompilerParams(vmem_limit_bytes=48 * 1024 * 1024),
        cost_estimate=pl.CostEstimate(
            flops=10 * rows * width * units,
            bytes_accessed=10 * width * units + 12 * rows * width,
            transcendentals=rows * units,
        ),
    )(z, z, wg, wu, wd)


def pack(rows):
    blocks = rows.shape[0] // CAP
    width = rows.shape[1]
    main = rows[: blocks * MAIN]
    extra = rows[blocks * MAIN :].reshape(blocks * MAIN, width // MAIN)
    return jnp.concatenate([main, extra], axis=1)


def unpack(packed, width):
    main = packed[:, :width]
    extra = packed[:, width:].reshape(packed.shape[0] // MAIN, width)
    return jnp.concatenate([main, extra], axis=0)


def visit_order(experts):
    order = [0]
    for k in range(1, experts // 2 + 1):
        order.append(k)
        if experts - k != k:
            order.append(experts - k)
    return order


def enter(me, pe, experts, neighbours):
    barrier = pltpu.get_barrier_semaphore()
    for k in range(1, experts):
        pl.semaphore_signal(
            barrier,
            inc=1,
            device_id=(me, lax.rem(pe + k, experts)),
            device_id_type=pl.DeviceIdType.MESH,
        )
    for other in neighbours:
        pl.semaphore_signal(
            barrier, inc=1, device_id=(other, pe), device_id_type=pl.DeviceIdType.MESH
        )
    pl.semaphore_wait(barrier, experts - 1 + len(neighbours))


def remote(src, dst, sems, slot, device):
    return pltpu.make_async_remote_copy(
        src_ref=src,
        dst_ref=dst,
        send_sem=sems.at[0, slot],
        recv_sem=sems.at[1, slot],
        device_id=device,
        device_id_type=pl.DeviceIdType.MESH,
    )


def dispatch_kernel(experts, send, got, own_sem, z_sem, x_sem, y_sem, xy_sem, yx_sem):
    me, pe = lax.axis_index("dp"), lax.axis_index("expert")
    along_x = me + 1 - 2 * lax.rem(me, 2)
    along_y = lax.rem(me + 2, DP)
    half = send.shape[2] // 2
    first, last = pl.ds(0, half), pl.ds(half, half)
    enter(me, pe, experts, (along_x, along_y))
    own = pltpu.make_async_copy(send.at[pe], got.at[0, pe], own_sem)
    own.start()
    order = visit_order(experts)
    across = {}
    for k in order[1:]:
        to = lax.rem(pe + k, experts)
        across[k] = remote(send.at[to], got.at[0, pe], z_sem, k, (me, to))
        across[k].start()
    copies = {}
    for step in range(experts + 1):
        if step < experts:
            k = order[step]
            block = lax.rem(pe + experts - k, experts)
            if k == 0:
                source = send.at[pe]
            else:
                across[k].wait_recv()
                source = got.at[0, block]
            ways = (
                remote(source, got.at[1, block], x_sem, k, (along_x, pe)),
                remote(source, got.at[2, block], y_sem, k, (along_y, pe)),
            )
            for way in ways:
                way.start()
            copies[k] = list(ways)
        if step >= 1:
            k = order[step - 1]
            block = lax.rem(pe + experts - k, experts)
            copies[k][0].wait_recv()
            onward = remote(
                got.at[1, block, :, first], got.at[3, block, :, first], xy_sem, k, (along_y, pe)
            )
            onward.start()
            copies[k].append(onward)
            copies[k][1].wait_recv()
            onward = remote(
                got.at[2, block, :, last], got.at[3, block, :, last], yx_sem, k, (along_x, pe)
            )
            onward.start()
            copies[k].append(onward)
    own.wait()
    for k in order:
        if k != 0:
            across[k].wait_send()
        for copy in copies[k]:
            copy.wait_send()
        copies[k][2].wait_recv()
        copies[k][3].wait_recv()


def dispatch(send):
    experts = send.shape[0]
    pairs = pltpu.SemaphoreType.DMA((2, experts))
    size = send.size * send.dtype.itemsize
    return pl.pallas_call(
        functools.partial(dispatch_kernel, experts),
        out_shape=jax.ShapeDtypeStruct((DP,) + send.shape, send.dtype),
        in_specs=[pl.BlockSpec(memory_space=pl.ANY)],
        out_specs=pl.BlockSpec(memory_space=pl.ANY),
        scratch_shapes=[pltpu.SemaphoreType.DMA(())] + [pairs] * 5,
        compiler_params=pltpu.CompilerParams(collective_id=0, has_side_effects=True),
        cost_estimate=pl.CostEstimate(flops=0, bytes_accessed=8 * size, transcendentals=0),
    )(send)


def return_kernel(
    experts, chunks, p, got, from_x, from_y, onward, last, ready, own_sem, s1_sem, s2_sem, z_sem
):
    f32, bf16 = jnp.float32, jnp.bfloat16
    me, pe = lax.axis_index("dp"), lax.axis_index("expert")
    along_x = me + 1 - 2 * lax.rem(me, 2)
    along_y = lax.rem(me + 2, DP)
    rows = p.shape[0] // DP
    wide = p.shape[1] // (2 * chunks)
    ways = ((along_x, along_y, 1, 2, from_x), (along_y, along_x, 2, 1, from_y))

    def part(r, half, c):
        return p.at[r * rows : (r + 1) * rows, pl.ds((half * chunks + c) * wide, wide)]

    enter(me, pe, experts, (along_x, along_y))
    first, second, across, own = {}, {}, [], []
    for c in range(chunks):
        for half, (to, _, near, _, land) in enumerate(ways):
            for i, r in enumerate((3, near)):
                slot = (c * 2 + half) * 2 + i
                first[c, half, i] = remote(
                    part(r, half, c), land.at[c, i], s1_sem, slot, (to, pe)
                )
                first[c, half, i].start()
    for c in range(chunks + 1):
        if c < chunks:
            for half, (_, to, _, pass_on, land) in enumerate(ways):
                first[c, half, 0].wait_recv()
                value = part(pass_on, half, c)[...].astype(f32) + land[c, 0].astype(f32)
                onward[c, half] = value.astype(bf16)
                second[c, half] = remote(
                    onward.at[c, half], last.at[c, half], s2_sem, c * 2 + half, (to, pe)
                )
                second[c, half].start()
        if c >= 1:
            d = c - 1
            totals = []
            for half, (_, _, _, _, land) in enumerate(ways):
                first[d, half, 1].wait_recv()
                second[d, half].wait_recv()
                total = part(0, half, d)[...].astype(f32) + land[d, 1].astype(f32)
                total = total + last[d, half].astype(f32)
                totals.append(total.reshape(experts, MAIN, wide))
            ready[d] = jnp.concatenate(totals, axis=1).astype(bf16)
            for k in visit_order(experts)[1:]:
                to = lax.rem(pe + k, experts)
                across.append(
                    remote(ready.at[d, to], got.at[d, pe], z_sem, d * experts + k, (me, to))
                )
                across[-1].start()
            own.append(pltpu.make_async_copy(ready.at[d, pe], got.at[d, pe], own_sem.at[d]))
            own[-1].start()
    for copy in list(first.values()) + list(second.values()):
        copy.wait_send()
    for copy in own + across:
        copy.wait()


def return_slots(p, experts):
    chunks = 2
    rows, wide = p.shape[0] // DP, p.shape[1] // (2 * chunks)
    landing = pltpu.VMEM((chunks, 2, rows, wide), p.dtype)
    size = rows * p.shape[1] * p.dtype.itemsize
    got = pl.pallas_call(
        functools.partial(return_kernel, experts, chunks),
        out_shape=jax.ShapeDtypeStruct((chunks, experts, 2 * MAIN, wide), p.dtype),
        in_specs=[pl.BlockSpec(memory_space=pltpu.VMEM)],
        out_specs=pl.BlockSpec(memory_space=pl.ANY),
        scratch_shapes=[landing] * 4
        + [
            pltpu.VMEM((chunks, experts, 2 * MAIN, wide), p.dtype),
            pltpu.SemaphoreType.DMA((chunks,)),
            pltpu.SemaphoreType.DMA((2, 4 * chunks)),
            pltpu.SemaphoreType.DMA((2, 2 * chunks)),
            pltpu.SemaphoreType.DMA((2, chunks * experts)),
        ],
        compiler_params=pltpu.CompilerParams(
            collective_id=1, has_side_effects=True, vmem_limit_bytes=48 * 1024 * 1024
        ),
        cost_estimate=pl.CostEstimate(flops=0, bytes_accessed=8 * size, transcendentals=0),
    )(p)
    got = got.reshape(chunks, experts, 2, MAIN, wide).transpose(1, 3, 2, 0, 4)
    return got.reshape(experts * MAIN, p.shape[1])


def shards(tokens, out_grad, expert_ids, gate_weights, w_gate, w_up, w_down):
    experts = lax.axis_size("expert")
    width = tokens.shape[1]
    bf16, f32 = jnp.bfloat16, jnp.float32
    place, scaled = slot_tables(expert_ids, gate_weights, experts)
    place_bf = place.astype(bf16)
    send_x = jnp.dot(place_bf, tokens, preferred_element_type=f32).astype(bf16)
    send_dy = jnp.dot(scaled, out_grad.astype(f32), precision=lax.Precision.HIGHEST).astype(bf16)
    both = [pack(rows).reshape(experts, MAIN, -1) for rows in (send_x, send_dy)]
    got = dispatch(jnp.concatenate(both, axis=1))
    z = got.reshape(DP * experts * 2 * MAIN, -1)
    slot_x, slot_dy, act, d_gate, d_up, partial = expert_block(z, w_gate[0], w_up[0], w_down[0])
    returned = unpack(return_slots(partial, experts), width)
    gate_grad = lax.dot_general(slot_x, d_gate, OVER_ROWS, preferred_element_type=f32).astype(bf16)
    up_grad = lax.dot_general(slot_x, d_up, OVER_ROWS, preferred_element_type=f32).astype(bf16)
    down_grad = lax.dot_general(act, slot_dy, OVER_ROWS, preferred_element_type=f32).astype(bf16)
    token_grad = lax.dot_general(place_bf, returned, OVER_ROWS, preferred_element_type=f32)
    return (token_grad.astype(bf16), gate_grad[None], up_grad[None], down_grad[None])


def solution(mesh):
    return jax.shard_map(
        shards,
        mesh=mesh,
        in_specs=(
            P(("dp", "expert"), None),
            P(("dp", "expert"), None),
            P(("dp", "expert"), None),
            P(("dp", "expert"), None),
            P("expert", None, "dp"),
            P("expert", None, "dp"),
            P("expert", "dp", None),
        ),
        out_specs=(
            P(("dp", "expert"), None),
            P("expert", None, "dp"),
            P("expert", None, "dp"),
            P("expert", "dp", None),
        ),
        check_vma=False,
    )
```

```python
import functools

import jax
import jax.numpy as jnp
from jax import lax
from jax.experimental import pallas as pl
from jax.experimental.pallas import tpu as pltpu
from jax.sharding import PartitionSpec as P

CAP = 9
MAIN = 8
DP = 4
OVER_ROWS = (((0,), (0,)), ((), ()))
OVER_UNITS = (((1,), (1,)), ((), ()))


def slot_tables(expert_ids, gate_weights, experts):
    tok_rows = expert_ids.shape[0]
    f32, bf16 = jnp.float32, jnp.bfloat16
    named = expert_ids.T[None, :, :] == jnp.arange(experts, dtype=jnp.int32)[:, None, None]
    member = jnp.sum(named.astype(f32), axis=1)
    weight = jnp.sum(jnp.where(named, gate_weights.T[None, :, :], f32(0.0)), axis=1)
    token = jnp.arange(tok_rows, dtype=jnp.int32)
    earlier = (token[:, None] < token[None, :]).astype(bf16)
    rank = jnp.dot(member.astype(bf16), earlier, preferred_element_type=f32)
    rank = jnp.where(member > 0, rank, f32(-1.0))

    def spread(values):
        main = jnp.broadcast_to(values[:, None, :], (experts, MAIN, tok_rows))
        return jnp.concatenate([main.reshape(experts * MAIN, tok_rows), values], axis=0)

    row = jnp.arange(experts * CAP, dtype=jnp.int32)
    slot = jnp.where(row < experts * MAIN, row % MAIN, MAIN).astype(f32)
    hits = spread(rank) == slot[:, None]
    place = hits.astype(f32)
    scaled = jnp.where(hits, spread(weight), f32(0.0))
    return (place, scaled)


def one_hot(shape, column_of_row, dim=0):
    along = lax.broadcasted_iota(jnp.int32, shape, dim)
    across = lax.broadcasted_iota(jnp.int32, shape, 1 - dim)
    return (column_of_row(along) == across).astype(jnp.bfloat16)


def expert_kernel(
    z, z_extra, wg, wu, wd, x, dy, act, d_gate, d_up, partial, gate_sum, up_sum, act_sum, extra_sum
):
    f32, bf16 = jnp.float32, jnp.bfloat16
    step = pl.program_id(0)
    rows2 = z.shape[0]
    main = rows2 // 2
    blocks = main // MAIN

    def dot(a, b, dims=(((1,), (0,)), ((), ()))):
        return lax.dot_general(a, b, dims, preferred_element_type=f32)

    @pl.when(step == 0)
    def _():
        for total in (gate_sum, up_sum, act_sum):
            total[...] = jnp.zeros_like(total)

    @pl.when(step < MAIN)
    def _():
        for out, offset in ((x, 0), (dy, MAIN)):
            pick = one_hot((main, rows2), lambda r: (r // MAIN) * 2 * MAIN + r % MAIN + offset)
            out[:main, :] = dot(pick, z[...]).astype(bf16)
            pick = one_hot((blocks, rows2), lambda r: r * 2 * MAIN + offset + step)
            out[main:, :] = dot(pick, z_extra[...]).astype(bf16)
        gate_sum[...] += dot(x[...], wg[...])
        up_sum[...] += dot(x[...], wu[...])
        act_sum[...] += dot(dy[...], wd[...], OVER_UNITS)

    @pl.when(step == MAIN - 1)
    def _():
        gate, up, d_act = gate_sum[...], up_sum[...], act_sum[...]
        sig = jax.nn.sigmoid(gate)
        act[...] = (gate * sig * up).astype(bf16)
        d_up[...] = (d_act * gate * sig).astype(bf16)
        d_gate[...] = (d_act * up * sig * (1.0 + gate * (1.0 - sig))).astype(bf16)
        extra_sum[...] = jnp.zeros_like(extra_sum)

    @pl.when((step >= MAIN) & (step < 2 * MAIN))
    def _():
        value = dot(d_gate[...], wg[...], OVER_UNITS) + dot(d_up[...], wu[...], OVER_UNITS)
        value = value.astype(bf16)
        partial[...] = value[:main]
        put = one_hot((main, blocks), lambda r: r * MAIN + (step - MAIN), 1)
        extra_sum[...] += dot(put, value[main:])

    @pl.when(step == 2 * MAIN)
    def _():
        partial[...] = extra_sum[...].astype(bf16)


def expert_block(z, wg, wu, wd):
    f32, bf16 = jnp.float32, jnp.bfloat16
    rows2, packed = z.shape
    width, units = wg.shape
    piece = width // MAIN
    main = rows2 // 2
    rows = main // MAIN * CAP

    def forth(i):
        return jnp.minimum(i, MAIN - 1)

    def both(i):
        return jnp.where(i < MAIN, i, jnp.minimum(i - MAIN, MAIN - 1))

    def after(i):
        return jnp.maximum(i - MAIN, 0)

    wide = pl.BlockSpec((rows, piece), lambda i: (0, forth(i)))
    whole = pl.BlockSpec((rows, units), lambda i: (0, 0))
    sums = pltpu.VMEM((rows, units), f32)
    hidden = jax.ShapeDtypeStruct((rows, units), bf16)
    tall = jax.ShapeDtypeStruct((rows, width), bf16)
    return pl.pallas_call(
        expert_kernel,
        grid=(2 * MAIN + 1,),
        in_specs=[
            pl.BlockSpec((rows2, piece), lambda i: (0, forth(i))),
            pl.BlockSpec((rows2, piece), lambda i: (0, MAIN)),
            pl.BlockSpec((piece, units), lambda i: (both(i), 0)),
            pl.BlockSpec((piece, units), lambda i: (both(i), 0)),
            pl.BlockSpec((units, piece), lambda i: (0, forth(i))),
        ],
        out_specs=[wide, wide, whole, whole, whole]
        + [pl.BlockSpec((main, piece), lambda i: (0, after(i)))],
        out_shape=[tall, tall, hidden, hidden, hidden]
        + [jax.ShapeDtypeStruct((main, packed), bf16)],
        scratch_shapes=[sums, sums, sums, pltpu.VMEM((main, piece), f32)],
        compiler_params=pltpu.CompilerParams(vmem_limit_bytes=48 * 1024 * 1024),
        cost_estimate=pl.CostEstimate(
            flops=10 * rows * width * units,
            bytes_accessed=10 * width * units + 12 * rows * width,
            transcendentals=rows * units,
        ),
    )(z, z, wg, wu, wd)


def pack(rows):
    blocks = rows.shape[0] // CAP
    width = rows.shape[1]
    main = rows[: blocks * MAIN]
    extra = rows[blocks * MAIN :].reshape(blocks * MAIN, width // MAIN)
    return jnp.concatenate([main, extra], axis=1)


def unpack(packed, width):
    main = packed[:, :width]
    extra = packed[:, width:].reshape(packed.shape[0] // MAIN, width)
    return jnp.concatenate([main, extra], axis=0)


def swap(value, bit):
    return lax.ppermute(value, "dp", [(i, i ^ bit) for i in range(DP)])


def visit_order(experts):
    order = [0]
    for k in range(1, experts // 2 + 1):
        order.append(k)
        if experts - k != k:
            order.append(experts - k)
    return order


def enter(me, pe, experts, neighbours):
    barrier = pltpu.get_barrier_semaphore()
    for k in range(1, experts):
        pl.semaphore_signal(
            barrier,
            inc=1,
            device_id=(me, lax.rem(pe + k, experts)),
            device_id_type=pl.DeviceIdType.MESH,
        )
    for other in neighbours:
        pl.semaphore_signal(
            barrier, inc=1, device_id=(other, pe), device_id_type=pl.DeviceIdType.MESH
        )
    pl.semaphore_wait(barrier, experts - 1 + len(neighbours))


def remote(src, dst, sems, slot, device):
    return pltpu.make_async_remote_copy(
        src_ref=src,
        dst_ref=dst,
        send_sem=sems.at[0, slot],
        recv_sem=sems.at[1, slot],
        device_id=device,
        device_id_type=pl.DeviceIdType.MESH,
    )


def dispatch_kernel(experts, send, got, own_sem, z_sem, x_sem, y_sem, xy_sem, yx_sem):
    me, pe = lax.axis_index("dp"), lax.axis_index("expert")
    along_x = me + 1 - 2 * lax.rem(me, 2)
    along_y = lax.rem(me + 2, DP)
    half = send.shape[2] // 2
    first, last = pl.ds(0, half), pl.ds(half, half)
    enter(me, pe, experts, (along_x, along_y))
    own = pltpu.make_async_copy(send.at[pe], got.at[0, pe], own_sem)
    own.start()
    order = visit_order(experts)
    across = {}
    for k in order[1:]:
        to = lax.rem(pe + k, experts)
        across[k] = remote(send.at[to], got.at[0, pe], z_sem, k, (me, to))
        across[k].start()
    copies = {}
    for step in range(experts + 1):
        if step < experts:
            k = order[step]
            block = lax.rem(pe + experts - k, experts)
            if k == 0:
                source = send.at[pe]
            else:
                across[k].wait_recv()
                source = got.at[0, block]
            ways = (
                remote(source, got.at[1, block], x_sem, k, (along_x, pe)),
                remote(source, got.at[2, block], y_sem, k, (along_y, pe)),
            )
            for way in ways:
                way.start()
            copies[k] = list(ways)
        if step >= 1:
            k = order[step - 1]
            block = lax.rem(pe + experts - k, experts)
            copies[k][0].wait_recv()
            onward = remote(
                got.at[1, block, :, first], got.at[3, block, :, first], xy_sem, k, (along_y, pe)
            )
            onward.start()
            copies[k].append(onward)
            copies[k][1].wait_recv()
            onward = remote(
                got.at[2, block, :, last], got.at[3, block, :, last], yx_sem, k, (along_x, pe)
            )
            onward.start()
            copies[k].append(onward)
    own.wait()
    for k in order:
        if k != 0:
            across[k].wait_send()
        for copy in copies[k]:
            copy.wait_send()
        copies[k][2].wait_recv()
        copies[k][3].wait_recv()


def dispatch(send):
    experts = send.shape[0]
    pairs = pltpu.SemaphoreType.DMA((2, experts))
    size = send.size * send.dtype.itemsize
    return pl.pallas_call(
        functools.partial(dispatch_kernel, experts),
        out_shape=jax.ShapeDtypeStruct((DP,) + send.shape, send.dtype),
        in_specs=[pl.BlockSpec(memory_space=pl.ANY)],
        out_specs=pl.BlockSpec(memory_space=pl.ANY),
        scratch_shapes=[pltpu.SemaphoreType.DMA(())] + [pairs] * 5,
        compiler_params=pltpu.CompilerParams(collective_id=0, has_side_effects=True),
        cost_estimate=pl.CostEstimate(flops=0, bytes_accessed=8 * size, transcendentals=0),
    )(send)


def exchange_kernel(experts, send, got, own_sem, z_sem):
    me, pe = lax.axis_index("dp"), lax.axis_index("expert")
    enter(me, pe, experts, ())
    own = pltpu.make_async_copy(send.at[pe], got.at[pe], own_sem)
    own.start()
    across = []
    for k in visit_order(experts)[1:]:
        to = lax.rem(pe + k, experts)
        across.append(remote(send.at[to], got.at[pe], z_sem, k, (me, to)))
        across[-1].start()
    own.wait()
    for copy in across:
        copy.wait()


def exchange(send):
    experts = send.shape[0]
    size = send.size * send.dtype.itemsize
    return pl.pallas_call(
        functools.partial(exchange_kernel, experts),
        out_shape=jax.ShapeDtypeStruct(send.shape, send.dtype),
        in_specs=[pl.BlockSpec(memory_space=pl.ANY)],
        out_specs=pl.BlockSpec(memory_space=pl.ANY),
        scratch_shapes=[pltpu.SemaphoreType.DMA(()), pltpu.SemaphoreType.DMA((2, experts))],
        compiler_params=pltpu.CompilerParams(collective_id=1, has_side_effects=True),
        cost_estimate=pl.CostEstimate(flops=0, bytes_accessed=4 * size, transcendentals=0),
    )(send)


def reduce_to_own(parts):
    rows = parts.shape[0] // DP
    half = parts.shape[1] // 2
    f32 = jnp.float32
    p = [parts[r * rows : (r + 1) * rows] for r in range(DP)]

    def way(cols, first, second):
        got = swap(jnp.concatenate([p[first][:, cols], p[3][:, cols]], axis=0), first)
        onward = p[second][:, cols].astype(f32) + got[rows:].astype(f32)
        last = swap(onward.astype(jnp.bfloat16), second)
        return p[0][:, cols].astype(f32) + got[:rows].astype(f32) + last.astype(f32)

    a = way(slice(0, half), 1, 2)
    b = way(slice(half, 2 * half), 2, 1)
    return jnp.concatenate([a, b], axis=1).astype(jnp.bfloat16)


def shards(tokens, out_grad, expert_ids, gate_weights, w_gate, w_up, w_down):
    experts = lax.axis_size("expert")
    width = tokens.shape[1]
    bf16, f32 = jnp.bfloat16, jnp.float32
    place, scaled = slot_tables(expert_ids, gate_weights, experts)
    place_bf = place.astype(bf16)
    send_x = jnp.dot(place_bf, tokens, preferred_element_type=f32).astype(bf16)
    send_dy = jnp.dot(scaled, out_grad.astype(f32), precision=lax.Precision.HIGHEST).astype(bf16)
    both = [pack(rows).reshape(experts, MAIN, -1) for rows in (send_x, send_dy)]
    got = dispatch(jnp.concatenate(both, axis=1))
    z = got.reshape(DP * experts * 2 * MAIN, -1)
    slot_x, slot_dy, act, d_gate, d_up, partial = expert_block(z, w_gate[0], w_up[0], w_down[0])
    slot_grad = reduce_to_own(partial)
    gate_grad = lax.dot_general(slot_x, d_gate, OVER_ROWS, preferred_element_type=f32).astype(bf16)
    up_grad = lax.dot_general(slot_x, d_up, OVER_ROWS, preferred_element_type=f32).astype(bf16)
    down_grad = lax.dot_general(act, slot_dy, OVER_ROWS, preferred_element_type=f32).astype(bf16)
    slot_grad, gate_grad, up_grad, down_grad = lax.optimization_barrier(
        (slot_grad, gate_grad, up_grad, down_grad)
    )
    blocks = slot_grad.reshape(experts, MAIN, -1)
    half = blocks.shape[2] // 2
    back = exchange(jnp.concatenate([blocks[:, :, :half], blocks[:, :, half:]], axis=1))
    back = jnp.concatenate([back[:, :MAIN], back[:, MAIN:]], axis=2)
    returned = unpack(back.reshape(experts * MAIN, -1), width)
    token_grad = lax.dot_general(place_bf, returned, OVER_ROWS, preferred_element_type=f32)
    return (token_grad.astype(bf16), gate_grad[None], up_grad[None], down_grad[None])


def solution(mesh):
    return jax.shard_map(
        shards,
        mesh=mesh,
        in_specs=(
            P(("dp", "expert"), None),
            P(("dp", "expert"), None),
            P(("dp", "expert"), None),
            P(("dp", "expert"), None),
            P("expert", None, "dp"),
            P("expert", None, "dp"),
            P("expert", "dp", None),
        ),
        out_specs=(
            P(("dp", "expert"), None),
            P("expert", None, "dp"),
            P("expert", None, "dp"),
            P("expert", "dp", None),
        ),
        check_vma=False,
    )
```

```python
import functools

import jax
import jax.numpy as jnp
from jax import lax
from jax.experimental import pallas as pl
from jax.experimental.pallas import tpu as pltpu
from jax.sharding import PartitionSpec as P

CAP = 9
MAIN = 8
DP = 4
OVER_ROWS = (((0,), (0,)), ((), ()))
OVER_UNITS = (((1,), (1,)), ((), ()))


def slot_tables(expert_ids, gate_weights, experts):
    tok_rows = expert_ids.shape[0]
    f32, bf16 = jnp.float32, jnp.bfloat16
    named = expert_ids.T[None, :, :] == jnp.arange(experts, dtype=jnp.int32)[:, None, None]
    member = jnp.sum(named.astype(f32), axis=1)
    weight = jnp.sum(jnp.where(named, gate_weights.T[None, :, :], f32(0.0)), axis=1)
    token = jnp.arange(tok_rows, dtype=jnp.int32)
    earlier = (token[:, None] < token[None, :]).astype(bf16)
    rank = jnp.dot(member.astype(bf16), earlier, preferred_element_type=f32)
    rank = jnp.where(member > 0, rank, f32(-1.0))

    def spread(values):
        main = jnp.broadcast_to(values[:, None, :], (experts, MAIN, tok_rows))
        return jnp.concatenate([main.reshape(experts * MAIN, tok_rows), values], axis=0)

    row = jnp.arange(experts * CAP, dtype=jnp.int32)
    slot = jnp.where(row < experts * MAIN, row % MAIN, MAIN).astype(f32)
    hits = spread(rank) == slot[:, None]
    place = hits.astype(f32)
    scaled = jnp.where(hits, spread(weight), f32(0.0))
    return (place, scaled)


def one_hot(shape, column_of_row, dim=0):
    along = lax.broadcasted_iota(jnp.int32, shape, dim)
    across = lax.broadcasted_iota(jnp.int32, shape, 1 - dim)
    return (column_of_row(along) == across).astype(jnp.bfloat16)


def expert_kernel(
    z, z_extra, wg, wu, wd, x, dy, act, d_gate, d_up, partial, gate_sum, up_sum, act_sum, extra_sum, picks
):
    f32, bf16 = jnp.float32, jnp.bfloat16
    step = pl.program_id(0)
    rows2 = z.shape[0]
    main = rows2 // 2
    blocks = main // MAIN

    def dot(a, b, dims=(((1,), (0,)), ((), ()))):
        return lax.dot_general(a, b, dims, preferred_element_type=f32)

    @pl.when(step == 0)
    def _():
        for total in (gate_sum, up_sum, act_sum):
            total[...] = jnp.zeros_like(total)
        for i in range(2):
            picks[i] = one_hot(
                (main, rows2), lambda r: (r // MAIN) * 2 * MAIN + r % MAIN + i * MAIN
            )

    @pl.when(step < MAIN)
    def _():
        for out, offset in ((x, 0), (dy, MAIN)):
            out[:main, :] = dot(picks[offset // MAIN], z[...]).astype(bf16)
            pick = one_hot((blocks, rows2), lambda r: r * 2 * MAIN + offset + step)
            out[main:, :] = dot(pick, z_extra[...]).astype(bf16)
        gate_sum[...] += dot(x[...], wg[...])
        up_sum[...] += dot(x[...], wu[...])
        act_sum[...] += dot(dy[...], wd[...], OVER_UNITS)

    @pl.when(step == MAIN - 1)
    def _():
        gate, up, d_act = gate_sum[...], up_sum[...], act_sum[...]
        sig = jax.nn.sigmoid(gate)
        act[...] = (gate * sig * up).astype(bf16)
        d_up[...] = (d_act * gate * sig).astype(bf16)
        d_gate[...] = (d_act * up * sig * (1.0 + gate * (1.0 - sig))).astype(bf16)
        extra_sum[...] = jnp.zeros_like(extra_sum)

    @pl.when((step >= MAIN) & (step < 2 * MAIN))
    def _():
        value = dot(d_gate[...], wg[...], OVER_UNITS) + dot(d_up[...], wu[...], OVER_UNITS)
        value = value.astype(bf16)
        partial[...] = value[:main]
        put = one_hot((main, blocks), lambda r: r * MAIN + (step - MAIN), 1)
        extra_sum[...] += dot(put, value[main:])

    @pl.when(step == 2 * MAIN)
    def _():
        partial[...] = extra_sum[...].astype(bf16)


def expert_block(z, wg, wu, wd):
    f32, bf16 = jnp.float32, jnp.bfloat16
    rows2, packed = z.shape
    width, units = wg.shape
    piece = width // MAIN
    main = rows2 // 2
    rows = main // MAIN * CAP

    def forth(i):
        return jnp.minimum(i, MAIN - 1)

    def both(i):
        return jnp.where(i < MAIN, i, jnp.minimum(i - MAIN, MAIN - 1))

    def after(i):
        return jnp.maximum(i - MAIN, 0)

    wide = pl.BlockSpec((rows, piece), lambda i: (0, forth(i)))
    whole = pl.BlockSpec((rows, units), lambda i: (0, 0))
    sums = pltpu.VMEM((rows, units), f32)
    hidden = jax.ShapeDtypeStruct((rows, units), bf16)
    tall = jax.ShapeDtypeStruct((rows, width), bf16)
    return pl.pallas_call(
        expert_kernel,
        grid=(2 * MAIN + 1,),
        in_specs=[
            pl.BlockSpec((rows2, piece), lambda i: (0, forth(i))),
            pl.BlockSpec((rows2, piece), lambda i: (0, MAIN)),
            pl.BlockSpec((piece, units), lambda i: (both(i), 0)),
            pl.BlockSpec((piece, units), lambda i: (both(i), 0)),
            pl.BlockSpec((units, piece), lambda i: (0, forth(i))),
        ],
        out_specs=[wide, wide, whole, whole, whole]
        + [pl.BlockSpec((main, piece), lambda i: (0, after(i)))],
        out_shape=[tall, tall, hidden, hidden, hidden]
        + [jax.ShapeDtypeStruct((main, packed), bf16)],
        scratch_shapes=[sums, sums, sums, pltpu.VMEM((main, piece), f32)]
        + [pltpu.VMEM((2, main, rows2), bf16)],
        compiler_params=pltpu.CompilerParams(vmem_limit_bytes=48 * 1024 * 1024),
        cost_estimate=pl.CostEstimate(
            flops=10 * rows * width * units,
            bytes_accessed=10 * width * units + 12 * rows * width,
            transcendentals=rows * units,
        ),
    )(z, z, wg, wu, wd)


def pack(rows):
    blocks = rows.shape[0] // CAP
    width = rows.shape[1]
    main = rows[: blocks * MAIN]
    extra = rows[blocks * MAIN :].reshape(blocks * MAIN, width // MAIN)
    return jnp.concatenate([main, extra], axis=1)


def unpack(packed, width):
    main = packed[:, :width]
    extra = packed[:, width:].reshape(packed.shape[0] // MAIN, width)
    return jnp.concatenate([main, extra], axis=0)


def swap(value, bit):
    return lax.ppermute(value, "dp", [(i, i ^ bit) for i in range(DP)])


def visit_order(experts):
    order = [0]
    for k in range(1, experts // 2 + 1):
        order.append(k)
        if experts - k != k:
            order.append(experts - k)
    return order


def enter(me, pe, experts, neighbours):
    barrier = pltpu.get_barrier_semaphore()
    for k in range(1, experts):
        pl.semaphore_signal(
            barrier,
            inc=1,
            device_id=(me, lax.rem(pe + k, experts)),
            device_id_type=pl.DeviceIdType.MESH,
        )
    for other in neighbours:
        pl.semaphore_signal(
            barrier, inc=1, device_id=(other, pe), device_id_type=pl.DeviceIdType.MESH
        )
    pl.semaphore_wait(barrier, experts - 1 + len(neighbours))


def remote(src, dst, sems, slot, device):
    return pltpu.make_async_remote_copy(
        src_ref=src,
        dst_ref=dst,
        send_sem=sems.at[0, slot],
        recv_sem=sems.at[1, slot],
        device_id=device,
        device_id_type=pl.DeviceIdType.MESH,
    )


def dispatch_kernel(experts, send, got, own_sem, z_sem, x_sem, y_sem, xy_sem, yx_sem):
    me, pe = lax.axis_index("dp"), lax.axis_index("expert")
    along_x = me + 1 - 2 * lax.rem(me, 2)
    along_y = lax.rem(me + 2, DP)
    half = send.shape[2] // 2
    first, last = pl.ds(0, half), pl.ds(half, half)
    enter(me, pe, experts, (along_x, along_y))
    own = pltpu.make_async_copy(send.at[pe], got.at[0, pe], own_sem)
    own.start()
    order = visit_order(experts)
    across = {}
    for k in order[1:]:
        to = lax.rem(pe + k, experts)
        across[k] = remote(send.at[to], got.at[0, pe], z_sem, k, (me, to))
        across[k].start()
    copies = {}
    for step in range(experts + 1):
        if step < experts:
            k = order[step]
            block = lax.rem(pe + experts - k, experts)
            if k == 0:
                source = send.at[pe]
            else:
                across[k].wait_recv()
                source = got.at[0, block]
            ways = (
                remote(source, got.at[1, block], x_sem, k, (along_x, pe)),
                remote(source, got.at[2, block], y_sem, k, (along_y, pe)),
            )
            for way in ways:
                way.start()
            copies[k] = list(ways)
        if step >= 1:
            k = order[step - 1]
            block = lax.rem(pe + experts - k, experts)
            copies[k][0].wait_recv()
            onward = remote(
                got.at[1, block, :, first], got.at[3, block, :, first], xy_sem, k, (along_y, pe)
            )
            onward.start()
            copies[k].append(onward)
            copies[k][1].wait_recv()
            onward = remote(
                got.at[2, block, :, last], got.at[3, block, :, last], yx_sem, k, (along_x, pe)
            )
            onward.start()
            copies[k].append(onward)
    own.wait()
    for k in order:
        if k != 0:
            across[k].wait_send()
        for copy in copies[k]:
            copy.wait_send()
        copies[k][2].wait_recv()
        copies[k][3].wait_recv()


def dispatch(send):
    experts = send.shape[0]
    pairs = pltpu.SemaphoreType.DMA((2, experts))
    size = send.size * send.dtype.itemsize
    return pl.pallas_call(
        functools.partial(dispatch_kernel, experts),
        out_shape=jax.ShapeDtypeStruct((DP,) + send.shape, send.dtype),
        in_specs=[pl.BlockSpec(memory_space=pl.ANY)],
        out_specs=pl.BlockSpec(memory_space=pl.ANY),
        scratch_shapes=[pltpu.SemaphoreType.DMA(())] + [pairs] * 5,
        compiler_params=pltpu.CompilerParams(collective_id=0, has_side_effects=True),
        cost_estimate=pl.CostEstimate(flops=0, bytes_accessed=8 * size, transcendentals=0),
    )(send)


def exchange_kernel(experts, send, got, own_sem, z_sem):
    me, pe = lax.axis_index("dp"), lax.axis_index("expert")
    enter(me, pe, experts, ())
    own = pltpu.make_async_copy(send.at[pe], got.at[pe], own_sem)
    own.start()
    across = []
    for k in visit_order(experts)[1:]:
        to = lax.rem(pe + k, experts)
        across.append(remote(send.at[to], got.at[pe], z_sem, k, (me, to)))
        across[-1].start()
    own.wait()
    for copy in across:
        copy.wait()


def exchange(send):
    experts = send.shape[0]
    size = send.size * send.dtype.itemsize
    return pl.pallas_call(
        functools.partial(exchange_kernel, experts),
        out_shape=jax.ShapeDtypeStruct(send.shape, send.dtype),
        in_specs=[pl.BlockSpec(memory_space=pl.ANY)],
        out_specs=pl.BlockSpec(memory_space=pl.ANY),
        scratch_shapes=[pltpu.SemaphoreType.DMA(()), pltpu.SemaphoreType.DMA((2, experts))],
        compiler_params=pltpu.CompilerParams(collective_id=1, has_side_effects=True),
        cost_estimate=pl.CostEstimate(flops=0, bytes_accessed=4 * size, transcendentals=0),
    )(send)


def reduce_to_own(parts):
    rows = parts.shape[0] // DP
    half = parts.shape[1] // 2
    f32 = jnp.float32
    p = [parts[r * rows : (r + 1) * rows] for r in range(DP)]

    def way(cols, first, second):
        got = swap(jnp.concatenate([p[first][:, cols], p[3][:, cols]], axis=0), first)
        onward = p[second][:, cols].astype(f32) + got[rows:].astype(f32)
        last = swap(onward.astype(jnp.bfloat16), second)
        return p[0][:, cols].astype(f32) + got[:rows].astype(f32) + last.astype(f32)

    a = way(slice(0, half), 1, 2)
    b = way(slice(half, 2 * half), 2, 1)
    return jnp.concatenate([a, b], axis=1).astype(jnp.bfloat16)


def shards(tokens, out_grad, expert_ids, gate_weights, w_gate, w_up, w_down):
    experts = lax.axis_size("expert")
    width = tokens.shape[1]
    bf16, f32 = jnp.bfloat16, jnp.float32
    place, scaled = slot_tables(expert_ids, gate_weights, experts)
    place_bf = place.astype(bf16)
    send_x = jnp.dot(place_bf, tokens, preferred_element_type=f32).astype(bf16)
    send_dy = jnp.dot(scaled, out_grad.astype(f32), precision=lax.Precision.HIGHEST).astype(bf16)
    both = [pack(rows).reshape(experts, MAIN, -1) for rows in (send_x, send_dy)]
    got = dispatch(jnp.concatenate(both, axis=1))
    z = got.reshape(DP * experts * 2 * MAIN, -1)
    slot_x, slot_dy, act, d_gate, d_up, partial = expert_block(z, w_gate[0], w_up[0], w_down[0])
    slot_grad = reduce_to_own(partial)
    gate_grad = lax.dot_general(slot_x, d_gate, OVER_ROWS, preferred_element_type=f32).astype(bf16)
    up_grad = lax.dot_general(slot_x, d_up, OVER_ROWS, preferred_element_type=f32).astype(bf16)
    down_grad = lax.dot_general(act, slot_dy, OVER_ROWS, preferred_element_type=f32).astype(bf16)
    slot_grad, gate_grad, up_grad, down_grad = lax.optimization_barrier(
        (slot_grad, gate_grad, up_grad, down_grad)
    )
    blocks = slot_grad.reshape(experts, MAIN, -1)
    half = blocks.shape[2] // 2
    back = exchange(jnp.concatenate([blocks[:, :, :half], blocks[:, :, half:]], axis=1))
    back = jnp.concatenate([back[:, :MAIN], back[:, MAIN:]], axis=2)
    returned = unpack(back.reshape(experts * MAIN, -1), width)
    token_grad = lax.dot_general(place_bf, returned, OVER_ROWS, preferred_element_type=f32)
    return (token_grad.astype(bf16), gate_grad[None], up_grad[None], down_grad[None])


def solution(mesh):
    return jax.shard_map(
        shards,
        mesh=mesh,
        in_specs=(
            P(("dp", "expert"), None),
            P(("dp", "expert"), None),
            P(("dp", "expert"), None),
            P(("dp", "expert"), None),
            P("expert", None, "dp"),
            P("expert", None, "dp"),
            P("expert", "dp", None),
        ),
        out_specs=(
            P(("dp", "expert"), None),
            P("expert", None, "dp"),
            P("expert", None, "dp"),
            P("expert", "dp", None),
        ),
        check_vma=False,
    )
```
